32 devices in a mesh: segment: 2 (over core), expert: 16 (over z, y, x).
Axes of the slice: x: 2, y: 2, z: 4, core: 2. Of those that a mesh axis runs over, the one named last changes fastest.
Arguments:
- fwd_tokens: bfloat16 [2048, 2048], P(('segment', 'expert')), may hold values from -6 to 6
- fwd_routes: int32 [2048, 8], P(('segment', 'expert')), may hold values from 0 to 15, all different within a row; in each aligned block of 64 rows (0 to 63, 64 to 127, ...) at most 36 rows name the same one
- fwd_gates: int32 [2048, 8], P(('segment', 'expert')), may hold values from 16 to 255
- bwd_tokens: bfloat16 [2048, 2048], P(('segment', 'expert')), may hold values from -6 to 6
- bwd_routes: int32 [2048, 8], P(('segment', 'expert')), may hold values from 0 to 15, all different within a row; in each aligned block of 64 rows (0 to 63, 64 to 127, ...) at most 36 rows name the same one
- bwd_gates: int32 [2048, 8], P(('segment', 'expert')), may hold values from 16 to 255
- bwd_cotangent: bfloat16 [2048, 2048], P(('segment', 'expert')), may hold values from -6 to 6
- norm_gain: float32 [2, 2048], P('segment'), may hold values from 0.1 to 1.9
- weight_in: bfloat16 [2, 16, 2048, 1536], P('segment', 'expert'), may hold values from -0.125 to 0.125
- weight_out: bfloat16 [2, 16, 768, 2048], P('segment', 'expert'), may hold values from -0.21875 to 0.21875
Outputs:
- passed_forward: bfloat16 [2048, 2048], P(('segment', 'expert'))
- passed_backward: bfloat16 [2048, 2048], P(('segment', 'expert'))
The draws below stay inside these ranges and needn't reach their ends.
Inputs may be any that keep to these rules, and one draw needn't show every extreme that they name: `fwd_routes`: each row names 8 different experts. Among the 64 rows of one device no expert is named more than 36 times, and in every draw some expert is named exactly 36 times by one device's rows. `bwd_routes`: as for fwd_routes.
All inputs are finite; a program needn't handle non-finite values.
Results may differ from the reference program's by a relative error of at most 0.0063.
Values may be sent and summed in bfloat16 or wider, within the bound.
A program may use at most 128 MiB of HBM per device.

```python
import math
import jax
import jax.numpy as jnp
import numpy as np
from jax import lax

D = 2048
FF = 768
TOP = 8
TOK_DEV = 64
EXPERTS = 16
MOST = 36
TOKENS = 2048
N_SEGMENT = 2
N_EXPERT = 16


def plant(drawn, stream_key, low, high):
    dims = drawn.shape
    spot = [jax.random.randint(jax.random.fold_in(stream_key, axis), (), 0, dims[axis]) for axis in range(len(dims))]
    drawn = drawn.at[tuple(spot)].set(low)
    longest = dims.index(max(dims))
    spot[longest] = (spot[longest] + 1) % dims[longest]
    return drawn.at[tuple(spot)].set(high)


def level_of(key, extent, cuts, smallest, top_value):
    loudness, own = 1.0, jax.random.fold_in(key, 6)
    for position, parts in cuts:
        heights = jnp.exp(jax.random.uniform(jax.random.fold_in(own, position), (parts,), jnp.float32, smallest / len(cuts), top_value / len(cuts)))
        loudness = loudness * jnp.repeat(heights, extent[position] // parts).reshape([-1 if axis == position else 1 for axis in range(len(extent))])
    return loudness


def routed_block(key, own, number, rows, number_of, top, bound, skew):
    sequence = jax.random.permutation(key, number_of)
    packed, common = load_shares(number_of, rows * top, bound, skew, True), load_shares(number_of, rows * top, bound, skew, False)
    places = jnp.arange(number_of)

    def named(lengths, offset_by):
        used = int((lengths > 0).sum())
        fixed = max(1, used // 4)
        shifted = fixed + (places - fixed + offset_by * (used - fixed)) % max(1, number_of - fixed)
        return jnp.zeros((number_of,), jnp.int32).at[sequence[jnp.where(places < fixed, places, shifted)]].set(jnp.asarray(lengths, jnp.int32))

    lengths = jnp.where(number % 4 == 0, named(packed, number // 4), named(common, number - number // 4 - 1))
    mixed = jax.random.permutation(jax.random.fold_in(own, 3), number_of)
    donor, sink = mixed[0:number_of // 2 * 2:2], mixed[1:number_of // 2 * 2:2]
    slack = jnp.minimum(lengths[donor] - 1, bound - lengths[sink]) // 2
    slack = jnp.where((donor == sequence[0]) | (sink == sequence[0]) | (lengths[sink] == 0), 0, jnp.maximum(slack, 0))
    shifted = jax.random.randint(jax.random.fold_in(own, 4), (number_of // 2,), 0, 1 << 20) % (slack + 1)
    lengths = lengths.at[donor].add(-shifted).at[sink].add(shifted)
    labels = jnp.searchsorted(jnp.cumsum(lengths), jnp.arange(rows * top), side="right").astype(jnp.int32)
    listing = labels.reshape(top, rows).T
    listing = listing[jax.random.permutation(jax.random.fold_in(own, 1), rows)]
    offset_by = jax.random.randint(jax.random.fold_in(own, 2), (rows, 1), 0, top)
    return jnp.take_along_axis(listing, (jnp.arange(top)[None, :] + offset_by) % top, axis=1)


def load_shares(amount, total, limit, lean, full):
    weights = [(1 << 20) // math.isqrt(standing ** lean) + 1 for standing in range(1, amount + 1)]
    largest = limit if full else min(limit, max(-(-total // amount), total * weights[0] // sum(weights)))
    least = 1 if total - largest >= amount - 1 else 0
    counts, spare = [largest] + [least] * (amount - 1), total - largest - least * (amount - 1)
    while spare > 0:
        movable = [i for i in range(1, amount) if counts[i] < largest] or [i for i in range(1, amount) if counts[i] < limit]
        mass, budget = sum([weights[i] for i in movable]), spare
        for i in movable:
            more = min(limit - counts[i], max(1, budget * weights[i] // mass), spare)
            counts[i] = counts[i] + more
            spare = spare - more
    return np.array(counts)


def scatter_about(own_key, extent, scale, bound, split=(), held_as=jnp.bfloat16):
    level = level_of(own_key, extent, split, -0.22, 0.18) if split else 1.0
    values = jax.random.normal(own_key, extent, jnp.float32) * scale * level
    return jnp.minimum(jnp.maximum(values, -bound), bound).astype(held_as)


def setup_inputs(seed: int = 0) -> dict:
    keys = jax.random.split(jax.random.key(seed), 11)
    fwd_tokens = scatter_about(keys[0], (TOKENS, D), 1.0, 6.0, ((0, 32),))
    fwd_routes_keys = jax.random.split(jax.random.fold_in(keys[1], 1), TOKENS // TOK_DEV)
    fwd_routes_turns = jax.random.permutation(jax.random.fold_in(keys[1], 3), TOKENS // TOK_DEV)
    fwd_routes = jax.vmap(lambda own, number: routed_block(jax.random.fold_in(keys[1], 2), own, number, TOK_DEV, EXPERTS, TOP, MOST, 2))(fwd_routes_keys, fwd_routes_turns).reshape((TOKENS, TOP))
    fwd_gates = plant(jax.random.randint(keys[2], (TOKENS, TOP), 16, 256), jax.random.fold_in(keys[2], 1), 16, 255).astype(jnp.int32)
    bwd_tokens = scatter_about(keys[3], (TOKENS, D), 1.0, 6.0, ((0, 32),))
    bwd_routes_keys = jax.random.split(jax.random.fold_in(keys[4], 1), TOKENS // TOK_DEV)
    bwd_routes_turns = jax.random.permutation(jax.random.fold_in(keys[4], 3), TOKENS // TOK_DEV)
    bwd_routes = jax.vmap(lambda own, number: routed_block(jax.random.fold_in(keys[4], 2), own, number, TOK_DEV, EXPERTS, TOP, MOST, 2))(bwd_routes_keys, bwd_routes_turns).reshape((TOKENS, TOP))
    bwd_gates = plant(jax.random.randint(keys[5], (TOKENS, TOP), 16, 256), jax.random.fold_in(keys[5], 1), 16, 255).astype(jnp.int32)
    bwd_cotangent = scatter_about(keys[6], (TOKENS, D), 1.0, 6.0, ((0, 32),))
    norm_gain = jnp.clip(1.0 + 0.18 * jax.random.normal(keys[7], (N_SEGMENT, D), jnp.float32), 0.1, 1.9)
    weight_in = scatter_about(keys[8], (N_SEGMENT, EXPERTS, D, 2 * FF), D ** -0.5, 0.125, ((0, 2), (1, 16)))
    weight_out = scatter_about(keys[9], (N_SEGMENT, EXPERTS, FF, D), FF ** -0.5, 0.21875, ((0, 2), (1, 16)))
    return dict(fwd_tokens=fwd_tokens, fwd_routes=fwd_routes, fwd_gates=fwd_gates, bwd_tokens=bwd_tokens, bwd_routes=bwd_routes, bwd_gates=bwd_gates, bwd_cotangent=bwd_cotangent, norm_gain=norm_gain, weight_in=weight_in, weight_out=weight_out)


eps = 1e-06

def rms_scale(values):
    return lax.rsqrt(lax.optimization_barrier(jnp.mean(values * values, axis=-1, keepdims=True)) + eps)

def expert_forward(in_rows, w_first, w_second):
    gate_up = jnp.dot(in_rows, w_first, preferred_element_type=jnp.float32)
    hidden_width = w_second.shape[0]
    hidden = (jax.nn.silu(gate_up[:, :hidden_width]) * gate_up[:, hidden_width:]).astype(jnp.bfloat16)
    return jnp.dot(hidden, w_second, preferred_element_type=jnp.float32).astype(jnp.bfloat16)

def expert_backward(in_rows, out_grad, w_first, w_second):
    gate_up = jnp.dot(in_rows, w_first, preferred_element_type=jnp.float32)
    hidden_width = w_second.shape[0]
    gate_part = gate_up[:, :hidden_width]
    up_part = gate_up[:, hidden_width:]
    sigmoid_gate = jax.nn.sigmoid(gate_part)
    activated = gate_part * sigmoid_gate
    slope = sigmoid_gate * (1.0 + gate_part * (1.0 - sigmoid_gate))
    hidden_grad = lax.dot_general(out_grad, w_second, (((1,), (1,)), ((), ())), preferred_element_type=jnp.float32)
    pre_grad = jnp.concatenate([hidden_grad * up_part * slope, hidden_grad * activated], axis=1).astype(jnp.bfloat16)
    return lax.dot_general(pre_grad, w_first, (((1,), (1,)), ((), ())), preferred_element_type=jnp.float32).astype(jnp.bfloat16)

def route_sum(in_rows, grad_rows, routes, gate_codes, w_first_all, w_second_all, with_grad):
    flat_routes = routes.reshape(-1).astype(jnp.int32)
    row_total = flat_routes.shape[0]
    tok_rows = in_rows.shape[0]
    width = in_rows.shape[1]
    padded_in = jnp.concatenate([in_rows, jnp.zeros((1, width), in_rows.dtype)], axis=0)
    padded_grad = jnp.concatenate([grad_rows, jnp.zeros((1, width), grad_rows.dtype)], axis=0)
    gate_flat = jnp.concatenate([gate_codes.reshape(-1).astype(jnp.float32) / 256.0, jnp.zeros((1,), jnp.float32)])
    slots = N_EXPERT * MOST

    def one_expert(total, items):
        expert_id, w_first, w_second = items
        picked = jnp.nonzero(flat_routes == expert_id, size=slots, fill_value=row_total)[0].astype(jnp.int32)
        token_ids = jnp.where(picked < row_total, picked // TOP, tok_rows).astype(jnp.int32)
        if with_grad:
            result = expert_backward(padded_in[token_ids], padded_grad[token_ids], w_first, w_second)
        else:
            result = expert_forward(padded_in[token_ids], w_first, w_second)
        contrib = gate_flat[picked][:, None] * result.astype(jnp.float32)
        return (total.at[token_ids].add(contrib), None)
    start = jnp.zeros((tok_rows + 1, width), jnp.float32)
    expert_ids = jnp.arange(EXPERTS, dtype=jnp.int32)
    total, _ = lax.scan(one_expert, start, (expert_ids, w_first_all, w_second_all))
    return total[:tok_rows]

def reference(fwd_tokens, fwd_routes, fwd_gates, bwd_tokens, bwd_routes, bwd_gates, bwd_cotangent, norm_gain, weight_in, weight_out):
    segment_rows = N_EXPERT * TOK_DEV
    forward_list = []
    backward_list = []
    for section in range(N_SEGMENT):
        lower = section * segment_rows
        upper = lower + segment_rows
        gain = norm_gain[section]
        fwd32 = fwd_tokens[lower:upper].astype(jnp.float32)
        fwd_normed = (fwd32 * rms_scale(fwd32) * gain).astype(jnp.bfloat16)
        fwd_moe = route_sum(fwd_normed, fwd_tokens[lower:upper], fwd_routes[lower:upper], fwd_gates[lower:upper], weight_in[section], weight_out[section], False)
        forward_list.append((fwd32 + fwd_moe).astype(jnp.bfloat16))
        bwd32 = bwd_tokens[lower:upper].astype(jnp.float32)
        bwd_scale = rms_scale(bwd32)
        bwd_base = bwd32 * bwd_scale
        bwd_normed = (bwd_base * gain).astype(jnp.bfloat16)
        cotangent = bwd_cotangent[lower:upper]
        norm_grad = route_sum(bwd_normed, cotangent, bwd_routes[lower:upper], bwd_gates[lower:upper], weight_in[section], weight_out[section], True)
        scaled = norm_grad * gain
        input_grad = cotangent.astype(jnp.float32) + bwd_scale * (scaled - bwd_base * lax.optimization_barrier(jnp.mean(scaled * bwd_base, axis=-1, keepdims=True)))
        backward_list.append(input_grad.astype(jnp.bfloat16))
    forward_all = jnp.stack(forward_list)
    backward_all = jnp.stack(backward_list)
    passed_forward = jnp.roll(forward_all, 1, axis=0).reshape(-1, D)
    passed_backward = jnp.roll(backward_all, -1, axis=0).reshape(-1, D)
    return (passed_forward, passed_backward)
```

```python
import functools

import jax
import jax.numpy as jnp
from jax import lax
from jax.experimental import pallas as pl
from jax.experimental.pallas import tpu as pltpu
from jax.sharding import PartitionSpec as P

eps = 1e-06
MESH = pl.DeviceIdType.MESH
BF = jnp.bfloat16
F32 = jnp.float32
GROUP = 4
BWD, FWD, COT = 0, 1, 2
NT = (((1,), (1,)), ((), ()))
TN = (((0,), (0,)), ((), ()))


def mm(a, b, dims=(((1,), (0,)), ((), ()))):
    return lax.dot_general(a, b, dims, preferred_element_type=F32)


def rms_scale(values):
    return lax.rsqrt(jnp.mean(values * values, axis=-1, keepdims=True) + eps)


def kernel(
    dims,
    fwd_tokens, fwd_routes, fwd_gates, bwd_tokens, bwd_routes, bwd_gates, cotangent, gain_ref,
    w_in_hbm, w_out_hbm,
    out_f, out_b,
    w_in, w_out, table, line_x, pack_x, recv_x, recv_r, recv_z, place, pre, own_sum, final,
    w_sem, tz_send, tz_recv, z_send, z_recv, p_send, p_recv, r_send, r_recv, s_send, s_recv,
    o_send, o_recv,
):
    n_seg, n_exp, cap, tile = dims
    n_line = n_exp // GROUP
    tok, width = fwd_tokens.shape
    chunks, cw = line_x.shape[1], line_x.shape[4]
    slots = pack_x.shape[3]
    ff = w_out.shape[0]
    top = fwd_routes.shape[1]
    seg = lax.axis_index("segment")
    me = lax.axis_index("expert")
    zi, j = me // GROUP, me % GROUP

    def line_peer(d):
        return lax.rem(zi + d, n_line)

    def plane_peer(d):
        return lax.rem(j + d, GROUP)

    def dev(s, z, p):
        return {"segment": s, "expert": z * GROUP + p}

    copies_w = [
        pltpu.make_async_copy(w_in_hbm, w_in, w_sem.at[0]),
        pltpu.make_async_copy(w_out_hbm, w_out, w_sem.at[1]),
    ]
    for copy in copies_w:
        copy.start()

    seg_steps = [1] if n_seg == 2 else [1, n_seg - 1]
    barrier = pltpu.get_barrier_semaphore()
    for d in range(1, n_line):
        pl.semaphore_signal(barrier, inc=1, device_id=dev(seg, line_peer(d), j), device_id_type=MESH)
    for d in range(1, GROUP):
        pl.semaphore_signal(barrier, inc=1, device_id=dev(seg, zi, plane_peer(d)), device_id_type=MESH)
    for d in seg_steps:
        pl.semaphore_signal(
            barrier, inc=1, device_id=dev(lax.rem(seg + d, n_seg), zi, j), device_id_type=MESH
        )

    lanes = table.shape[2]
    lane = lax.broadcasted_iota(jnp.int32, (tok, lanes), 1)
    earlier = (
        lax.broadcasted_iota(jnp.int32, (tok, tok), 1) < lax.broadcasted_iota(jnp.int32, (tok, tok), 0)
    )
    earlier = jnp.where(earlier, 1.0, 0.0).astype(BF)
    entries = jnp.zeros((tok, lanes), F32)
    for base, routes, gates in ((0, bwd_routes, bwd_gates), (2 * n_exp, fwd_routes, fwd_gates)):
        routed = jnp.zeros((tok, lanes), F32)
        gate = jnp.zeros((tok, lanes), F32)
        for k in range(top):
            name = routes[:, k : k + 1]
            code = gates[:, k : k + 1].astype(F32) * (1.0 / 256.0)
            routed = routed + jnp.where(lane == name + base, 1.0, 0.0)
            gate = gate + jnp.where(lane == name + (base + n_exp), code, 0.0)
        rank = jnp.where(routed > 0.5, mm(earlier, routed.astype(BF)), -65536.0)
        entries = jnp.where((lane >= base) & (lane < base + n_exp), rank, entries)
        entries = entries + gate
    table[zi] = entries

    gain = gain_ref[...]

    def put_line(a, rows):
        for c in range(chunks):
            line_x[a, c, zi] = rows[:, c * cw : (c + 1) * cw]

    def normed(ref):
        x = ref[...].astype(F32)
        return (x * rms_scale(x) * gain).astype(BF)

    put_line(BWD, normed(bwd_tokens))

    pl.semaphore_wait(barrier, n_line - 1 + GROUP - 1 + len(seg_steps))

    def table_copy(d, slot):
        return pltpu.make_async_remote_copy(
            table.at[slot], table.at[slot], tz_send.at[d], tz_recv.at[d],
            device_id=dev(seg, line_peer(d), j), device_id_type=MESH,
        )

    def line_copy(a, c, d, slot):
        return pltpu.make_async_remote_copy(
            line_x.at[a, c, slot], line_x.at[a, c, slot], z_send.at[a, c, d], z_recv.at[a, c, d],
            device_id=dev(seg, line_peer(d), j), device_id_type=MESH,
        )

    def pack_copy(a, c, d, slot):
        return pltpu.make_async_remote_copy(
            pack_x.at[a, c, plane_peer(d)], recv_x.at[a, c, slot], p_send.at[a, c, d], p_recv.at[a, c, d],
            device_id=dev(seg, zi, plane_peer(d)), device_id_type=MESH,
        )

    def result_copy(a, c, d, slot):
        return pltpu.make_async_remote_copy(
            pack_x.at[a, c, plane_peer(d)], recv_r.at[a, c, slot], r_send.at[a, c, d], r_recv.at[a, c, d],
            device_id=dev(seg, zi, plane_peer(d)), device_id_type=MESH,
        )

    def sum_copy(a, c, d):
        return pltpu.make_async_remote_copy(
            line_x.at[a, c, line_peer(d)], recv_z.at[a, c, d - 1], s_send.at[a, c, d], s_recv.at[a, c, d],
            device_id=dev(seg, line_peer(d), j), device_id_type=MESH,
        )

    line_from = lambda d: lax.rem(zi + n_line - d, n_line)
    plane_from = lambda d: lax.rem(j + GROUP - d, GROUP)

    for d in range(1, n_line):
        table_copy(d, zi).start()

    def send_line(a):
        for c in range(chunks):
            for d in range(1, n_line):
                line_copy(a, c, d, zi).start()

    send_line(BWD)
    put_line(COT, cotangent[...])
    send_line(COT)
    put_line(FWD, normed(fwd_tokens))
    send_line(FWD)

    for d in range(1, n_line):
        table_copy(d, line_from(d)).wait_recv()
    rows = n_line * tok
    listing = table[...].reshape(rows, lanes)
    all_lane = lax.broadcasted_iota(jnp.int32, (rows, lanes), 1)
    block = (lax.broadcasted_iota(jnp.int32, (rows, slots), 0) // tok * cap).astype(F32)
    slot_id = lax.broadcasted_iota(jnp.int32, (rows, slots), 1).astype(F32) - block

    def column(base):
        return jnp.sum(jnp.where(all_lane == base, listing, 0.0), axis=1, keepdims=True)

    for a, base in ((BWD, 0), (FWD, 2 * n_exp)):
        for d in range(GROUP):
            expert = zi * GROUP + plane_peer(d)
            placed = column(base + expert) == slot_id
            place[a, d] = jnp.where(placed, column(base + n_exp + expert), 0.0).astype(BF)

    for a in (BWD, COT, FWD):
        for c in range(chunks):
            for d in range(1, n_line):
                line_copy(a, c, d, line_from(d)).wait_recv()
            for d in list(range(1, GROUP)) + [0]:
                x = line_x[a, c].reshape(rows, cw)
                gates = place[FWD if a == FWD else BWD, d].astype(F32)
                chosen = jnp.where(gates > 0.0, 1.0, 0.0).astype(BF)
                packed = mm(chosen, x, TN).astype(BF)
                if d == 0:
                    recv_x[a, c, j] = packed
                else:
                    pack_x[a, c, plane_peer(d)] = packed
                    pack_copy(a, c, d, j).start()

    for copy in copies_w:
        copy.wait()
    for d in range(1, n_line):
        table_copy(d, zi).wait_send()

    def wait_packed(a):
        for c in range(chunks):
            for d in range(1, GROUP):
                pack_copy(a, c, d, plane_from(d)).wait_recv()

    def wait_pack_sent(a):
        for c in range(chunks):
            for d in range(1, GROUP):
                pack_copy(a, c, d, j).wait_send()

    many = GROUP * slots

    def in_dot(a, col):
        total = None
        for c in range(chunks):
            part = mm(
                recv_x[a, c].reshape(many, cw),
                w_in[c * cw : (c + 1) * cw, pl.ds(pl.multiple_of(col, tile), tile)],
            )
            total = part if total is None else total + part
        return total

    def send_results(a, c):
        for d in range(1, GROUP):
            result_copy(a, c, d, j).start()

    wait_packed(BWD)
    wait_packed(COT)

    @pl.loop(0, ff // tile)
    def _(t):
        at = pl.multiple_of(t * tile, tile)
        g = in_dot(BWD, at)
        u = in_dot(BWD, ff + at)
        grad = None
        for c in range(chunks):
            part = mm(
                recv_x[COT, c].reshape(many, cw), w_out[pl.ds(at, tile), c * cw : (c + 1) * cw], NT
            )
            grad = part if grad is None else grad + part
        sg = jax.nn.sigmoid(g)
        pre[:, pl.ds(at, tile)] = (grad * u * (sg * (1.0 + g * (1.0 - sg)))).astype(BF)
        pre[:, pl.ds(pl.multiple_of(ff + at, tile), tile)] = (grad * (g * sg)).astype(BF)

    wait_pack_sent(BWD)
    for c in range(chunks):

        @pl.loop(0, cw // tile)
        def _(t):
            at = pl.multiple_of(t * tile, tile)
            part = mm(pre[...], w_in[pl.ds(pl.multiple_of(c * cw + at, tile), tile), :], NT).astype(BF)
            pack_x[BWD, c, :, :, pl.ds(at, tile)] = part.reshape(GROUP, slots, tile)

        send_results(BWD, c)

    wait_packed(FWD)

    @pl.loop(0, ff // tile)
    def _(t):
        at = pl.multiple_of(t * tile, tile)
        g = in_dot(FWD, at)
        u = in_dot(FWD, ff + at)
        pre[:, pl.ds(at, tile)] = (jax.nn.silu(g) * u).astype(BF)

    wait_pack_sent(FWD)
    for c in range(chunks):

        @pl.loop(0, cw // tile)
        def _(t):
            at = pl.multiple_of(t * tile, tile)
            part = mm(pre[:, :ff], w_out[:, pl.ds(pl.multiple_of(c * cw + at, tile), tile)]).astype(BF)
            pack_x[FWD, c, :, :, pl.ds(at, tile)] = part.reshape(GROUP, slots, tile)

        send_results(FWD, c)
    wait_pack_sent(COT)

    for a in (BWD, COT, FWD):
        for c in range(chunks):
            for d in range(1, n_line):
                line_copy(a, c, d, zi).wait_send()

    for a in (BWD, FWD):
        for c in range(chunks):
            for d in range(1, GROUP):
                result_copy(a, c, d, plane_from(d)).wait_recv()

            @pl.loop(0, n_line)
            def _(z):
                at = pl.multiple_of(z * tok, tok)
                total = mm(place[a, 0, pl.ds(at, tok)], pack_x[a, c, j])
                for d in range(1, GROUP):
                    total = total + mm(place[a, d, pl.ds(at, tok)], recv_r[a, c, plane_peer(d)])
                line_x[a, c, z] = total.astype(BF)

                @pl.when(z == zi)
                def _():
                    own_sum[a, c] = total

            for d in range(1, n_line):
                sum_copy(a, c, d).start()

    def summed(a):
        parts = []
        for c in range(chunks):
            total = own_sum[a, c]
            for d in range(1, n_line):
                sum_copy(a, c, d).wait_recv()
                total = total + recv_z[a, c, d - 1].astype(F32)
            parts.append(total)
        return jnp.concatenate(parts, axis=1)

    def out_copy(a, out, step):
        return pltpu.make_async_remote_copy(
            final.at[a], out, o_send.at[a], o_recv.at[a],
            device_id=dev(lax.rem(seg + step, n_seg), zi, j), device_id_type=MESH,
        )

    norm_grad = summed(BWD)
    x = bwd_tokens[...].astype(F32)
    scale = rms_scale(x)
    based = x * scale
    scaled = norm_grad * gain
    final[BWD] = (
        cotangent[...].astype(F32)
        + scale * (scaled - based * jnp.mean(scaled * based, axis=-1, keepdims=True))
    ).astype(BF)
    back = out_copy(BWD, out_b, n_seg - 1)
    back.start()
    final[FWD] = (fwd_tokens[...].astype(F32) + summed(FWD)).astype(BF)
    onward = out_copy(FWD, out_f, 1)
    onward.start()

    for a in (BWD, FWD):
        for c in range(chunks):
            for d in range(1, GROUP):
                result_copy(a, c, d, j).wait_send()
            for d in range(1, n_line):
                sum_copy(a, c, d).wait_send()
    back.wait()
    onward.wait()


def local(sizes, fwd_tokens, fwd_routes, fwd_gates, bwd_tokens, bwd_routes, bwd_gates, cotangent,
          norm_gain, weight_in, weight_out):
    n_seg, n_exp = sizes
    tok, width = fwd_tokens.shape
    top = fwd_routes.shape[1]
    w_first, w_second = weight_in[0, 0], weight_out[0, 0]
    ff = w_second.shape[0]
    n_line = n_exp // GROUP
    cap = max(2, min(tok, 9 * tok * top // (8 * n_exp)))
    slots = -(-cap * n_line // 16) * 16
    chunks = 2
    cw = width // chunks
    tile = 256
    lanes = -(-4 * n_exp // 128) * 128
    vmem = pl.BlockSpec(memory_space=pltpu.VMEM)
    anyw = pl.BlockSpec(memory_space=pl.ANY)
    dma = pltpu.SemaphoreType.DMA
    many = GROUP * slots
    return pl.pallas_call(
        functools.partial(kernel, (n_seg, n_exp, cap, tile)),
        out_shape=[jax.ShapeDtypeStruct((tok, width), BF)] * 2,
        in_specs=[vmem] * 8 + [anyw] * 2,
        out_specs=[anyw] * 2,
        scratch_shapes=[
            pltpu.VMEM(w_first.shape, BF),
            pltpu.VMEM(w_second.shape, BF),
            pltpu.VMEM((n_line, tok, lanes), F32),
            pltpu.VMEM((3, chunks, n_line, tok, cw), BF),
            pltpu.VMEM((3, chunks, GROUP, slots, cw), BF),
            pltpu.VMEM((3, chunks, GROUP, slots, cw), BF),
            pltpu.VMEM((2, chunks, GROUP, slots, cw), BF),
            pltpu.VMEM((2, chunks, n_line - 1, tok, cw), BF),
            pltpu.VMEM((2, GROUP, n_line * tok, slots), BF),
            pltpu.VMEM((many, 2 * ff), BF),
            pltpu.VMEM((2, chunks, tok, cw), F32),
            pltpu.VMEM((2, tok, width), BF),
            dma((2,)),
            dma((n_line,)), dma((n_line,)),
            dma((3, chunks, n_line)), dma((3, chunks, n_line)),
            dma((3, chunks, GROUP)), dma((3, chunks, GROUP)),
            dma((2, chunks, GROUP)), dma((2, chunks, GROUP)),
            dma((2, chunks, n_line)), dma((2, chunks, n_line)),
            dma((2,)), dma((2,)),
        ],
        compiler_params=pltpu.CompilerParams(
            collective_id=0, has_side_effects=True, vmem_limit_bytes=62 * 1024 * 1024
        ),
        cost_estimate=pl.CostEstimate(
            flops=2 * many * width * ff * 8, bytes_accessed=2 * width * ff * 3, transcendentals=0
        ),
    )(fwd_tokens, fwd_routes, fwd_gates, bwd_tokens, bwd_routes, bwd_gates, cotangent, norm_gain,
      w_first, w_second)


def solution(mesh):
    rows = P(("segment", "expert"), None)
    placed = (rows,) * 7 + (
        P("segment", None),
        P("segment", "expert", None, None),
        P("segment", "expert", None, None),
    )
    return jax.shard_map(
        functools.partial(local, (mesh.shape["segment"], mesh.shape["expert"])),
        mesh=mesh,
        in_specs=placed,
        out_specs=(rows, rows),
        check_vma=False,
    )
```

```python
import functools

import jax
import jax.numpy as jnp
from jax import lax
from jax.experimental import pallas as pl
from jax.experimental.pallas import tpu as pltpu
from jax.sharding import PartitionSpec as P

eps = 1e-06
MESH = pl.DeviceIdType.MESH
BF = jnp.bfloat16
F32 = jnp.float32
GROUP = 4
BWD, FWD, COT = 0, 1, 2
NT = (((1,), (1,)), ((), ()))
TN = (((0,), (0,)), ((), ()))


def mm(a, b, dims=(((1,), (0,)), ((), ()))):
    return lax.dot_general(a, b, dims, preferred_element_type=F32)


def rms_scale(values):
    return lax.rsqrt(jnp.mean(values * values, axis=-1, keepdims=True) + eps)


def kernel(
    dims,
    fwd_tokens, fwd_routes, fwd_gates, bwd_tokens, bwd_routes, bwd_gates, cotangent, gain_ref,
    w_in_hbm, w_out_hbm,
    out_f, out_b,
    w_in, w_out, table, line_x, pack_x, recv_x, recv_r, recv_z, place, pre, own_sum, final, via,
    w_sem, tz_send, tz_recv, z_send, z_recv, f_send, p_send, p_recv, r_send, r_recv, s_send, s_recv,
    o_send, o_recv,
):
    n_seg, n_exp, cap, tile = dims
    n_line = n_exp // GROUP
    tok, width = fwd_tokens.shape
    chunks, cw = line_x.shape[1], line_x.shape[4]
    slots = pack_x.shape[3]
    ff = w_out.shape[0]
    top = fwd_routes.shape[0]
    half = n_line // 2
    hc = cw // 2
    seg = lax.axis_index("segment")
    me = lax.axis_index("expert")
    zi, j = me // GROUP, me % GROUP

    def line_peer(d):
        return lax.rem(zi + d, n_line)

    def plane_peer(d):
        x, y = lax.rem(j, 2), j // 2
        return lax.rem(y + d // 2, 2) * 2 + lax.rem(x + d % 2, 2)

    def dev(s, z, p):
        return {"segment": s, "expert": z * GROUP + p}

    copies_w = [
        pltpu.make_async_copy(w_in_hbm, w_in, w_sem.at[0]),
        pltpu.make_async_copy(w_out_hbm, w_out, w_sem.at[1]),
    ]
    for copy in copies_w:
        copy.start()

    seg_steps = [1] if n_seg == 2 else [1, n_seg - 1]
    barrier = pltpu.get_barrier_semaphore()
    for d in range(1, n_line):
        pl.semaphore_signal(barrier, inc=1, device_id=dev(seg, line_peer(d), j), device_id_type=MESH)
    for d in range(1, GROUP):
        pl.semaphore_signal(barrier, inc=1, device_id=dev(seg, zi, plane_peer(d)), device_id_type=MESH)
    for d in seg_steps:
        pl.semaphore_signal(
            barrier, inc=1, device_id=dev(lax.rem(seg + d, n_seg), zi, j), device_id_type=MESH
        )

    lanes = table.shape[2]
    line = lax.broadcasted_iota(jnp.int32, (lanes, tok), 0)
    earlier = (
        lax.broadcasted_iota(jnp.int32, (tok, tok), 0) < lax.broadcasted_iota(jnp.int32, (tok, tok), 1)
    )
    earlier = jnp.where(earlier, 1.0, 0.0).astype(BF)
    entries = jnp.zeros((lanes, tok), F32)
    for base, routes, gates in ((0, bwd_routes, bwd_gates), (2 * n_exp, fwd_routes, fwd_gates)):
        routed = jnp.zeros((lanes, tok), F32)
        gate = jnp.zeros((lanes, tok), F32)
        for k in range(top):
            name = routes[k : k + 1, :]
            code = gates[k : k + 1, :].astype(F32) * (1.0 / 256.0)
            routed = routed + jnp.where(line == name + base, 1.0, 0.0)
            gate = gate + jnp.where(line == name + (base + n_exp), code, 0.0)
        rank = jnp.where(routed > 0.5, mm(routed.astype(BF), earlier), -65536.0)
        entries = jnp.where((line >= base) & (line < base + n_exp), rank, entries)
        entries = entries + gate
    table[zi] = entries.T

    gain = gain_ref[...]

    def put_line(a, rows):
        for c in range(chunks):
            line_x[a, c, zi] = rows[:, c * cw : (c + 1) * cw]

    def normed(ref):
        x = ref[...].astype(F32)
        return (x * rms_scale(x) * gain).astype(BF)

    put_line(FWD, normed(fwd_tokens))

    pl.semaphore_wait(barrier, n_line - 1 + GROUP - 1 + len(seg_steps))

    def table_copy(d, slot):
        return pltpu.make_async_remote_copy(
            table.at[slot], table.at[slot], tz_send.at[d], tz_recv.at[d],
            device_id=dev(seg, line_peer(d), j), device_id_type=MESH,
        )

    side, place_in = zi // half, zi % half
    far = 1 - side
    gate_here = side * half + (half - 1) * (1 - side)
    gate_far = far * half + (half - 1) * (1 - far)

    def line_copy(a, c, slot, target, send_sem):
        return pltpu.make_async_remote_copy(
            line_x.at[a, c, slot], line_x.at[a, c, slot], send_sem, z_recv.at[a, c, slot],
            device_id=dev(seg, target, j), device_id_type=MESH,
        )

    def own_copies(a, c):
        found = [
            line_copy(a, c, zi, side * half + lax.rem(place_in + d, half), z_send.at[a, c, d])
            for d in range(1, half)
        ]
        return [line_copy(a, c, zi, gate_far, z_send.at[a, c, 0])] + found

    def onward_copy(a, c, b, d):
        target = side * half + lax.rem(place_in + d, half)
        return line_copy(a, c, far * half + b, target, f_send.at[a, c, b, d])

    def line_arrived(a, c):
        for b in range(half):
            slot = far * half + b
            line_copy(a, c, slot, zi, z_send.at[a, c, 0]).wait_recv()

            @pl.when(zi == gate_here)
            def _():
                for d in range(1, half):
                    onward_copy(a, c, b, d).start()

        for d in range(1, half):
            slot = side * half + lax.rem(place_in + d, half)
            line_copy(a, c, slot, zi, z_send.at[a, c, 0]).wait_recv()

    def line_sent(a, c):
        for copy in own_copies(a, c):
            copy.wait_send()

        @pl.when(zi == gate_here)
        def _():
            for b in range(half):
                for d in range(1, half):
                    onward_copy(a, c, b, d).wait_send()

    near, last = 1, 2

    def plane_copies(back, a, c, d):
        landing, sent, got = (recv_r, r_send, r_recv) if back else (recv_x, p_send, p_recv)
        src, dst = pack_x.at[a, c, plane_peer(d)], landing.at[a, c, j]
        if d < 3:
            return [
                pltpu.make_async_remote_copy(
                    src, dst, sent.at[a, c, d], got.at[a, c, d],
                    device_id=dev(seg, zi, plane_peer(d)), device_id_type=MESH,
                )
            ]
        return [
            pltpu.make_async_remote_copy(
                src.at[:, hc:], via.at[int(back), a, c], sent.at[a, c, 0], got.at[a, c, 0],
                device_id=dev(seg, zi, plane_peer(near)), device_id_type=MESH,
            ),
            pltpu.make_async_remote_copy(
                src.at[:, :hc], dst.at[:, :hc], sent.at[a, c, 3], got.at[a, c, 3],
                device_id=dev(seg, zi, plane_peer(3)), device_id_type=MESH,
            ),
        ]

    def via_copy(back, a, c):
        landing, sent, got = (recv_r, r_send, r_recv) if back else (recv_x, p_send, p_recv)
        return pltpu.make_async_remote_copy(
            via.at[int(back), a, c], landing.at[a, c, plane_peer(near), :, hc:],
            sent.at[a, c, 4], got.at[a, c, 4],
            device_id=dev(seg, zi, plane_peer(last)), device_id_type=MESH,
        )

    def pass_on(back, a, c):
        plane_copies(back, a, c, 3)[0].wait_recv()
        via_copy(back, a, c).start()

    def plane_wait(back, a, c):
        landing, sent, got = (recv_r, r_send, r_recv) if back else (recv_x, p_send, p_recv)
        for d in (1, 2):
            dst = landing.at[a, c, plane_peer(d)]
            pltpu.make_async_remote_copy(
                pack_x.at[a, c, plane_peer(d)], dst, sent.at[a, c, d], got.at[a, c, d],
                device_id=dev(seg, zi, plane_peer(d)), device_id_type=MESH,
            ).wait_recv()
        dst = landing.at[a, c, plane_peer(3)]
        pltpu.make_async_remote_copy(
            pack_x.at[a, c, plane_peer(3), :, :hc], dst.at[:, :hc], sent.at[a, c, 3], got.at[a, c, 3],
            device_id=dev(seg, zi, plane_peer(3)), device_id_type=MESH,
        ).wait_recv()
        pltpu.make_async_remote_copy(
            via.at[int(back), a, c], dst.at[:, hc:], sent.at[a, c, 4], got.at[a, c, 4],
            device_id=dev(seg, zi, plane_peer(last)), device_id_type=MESH,
        ).wait_recv()

    def plane_sent(back, a, c):
        for d in range(1, GROUP):
            for copy in plane_copies(back, a, c, d):
                copy.wait_send()

    def sum_copy(a, c, d):
        return pltpu.make_async_remote_copy(
            line_x.at[a, c, line_peer(d)], recv_z.at[a, c, d - 1], s_send.at[a, c, d], s_recv.at[a, c, d],
            device_id=dev(seg, line_peer(d), j), device_id_type=MESH,
        )

    line_from = lambda d: lax.rem(zi + n_line - d, n_line)
    plane_from = plane_peer

    for d in range(1, n_line):
        table_copy(d, zi).start()

    items = [(a, c) for a in (FWD, BWD, COT) for c in range(chunks)]

    def send_line(i):
        if i < len(items):
            for copy in own_copies(*items[i]):
                copy.start()

    send_line(0)
    send_line(1)
    put_line(BWD, normed(bwd_tokens))
    put_line(COT, cotangent[...])

    for d in range(1, n_line):
        table_copy(d, line_from(d)).wait_recv()
    rows = n_line * tok
    listing = table[...].reshape(rows, lanes)
    all_lane = lax.broadcasted_iota(jnp.int32, (rows, lanes), 1)
    block = (lax.broadcasted_iota(jnp.int32, (rows, slots), 0) // tok * cap).astype(F32)
    slot_id = lax.broadcasted_iota(jnp.int32, (rows, slots), 1).astype(F32) - block

    def column(base):
        return jnp.sum(jnp.where(all_lane == base, listing, 0.0), axis=1, keepdims=True)

    for a, base in ((BWD, 0), (FWD, 2 * n_exp)):
        for d in range(GROUP):
            expert = zi * GROUP + plane_peer(d)
            placed = column(base + expert) == slot_id
            place[a, d] = jnp.where(placed, column(base + n_exp + expert), 0.0).astype(BF)

    def wait_packed(a):
        for c in range(chunks):
            plane_wait(False, a, c)

    def wait_pack_sent(a):
        for c in range(chunks):
            plane_sent(False, a, c)
            via_copy(False, a, c).wait_send()

    many = GROUP * slots

    def in_dot(a, col):
        total = None
        for c in range(chunks):
            part = mm(
                recv_x[a, c].reshape(many, cw),
                w_in[c * cw : (c + 1) * cw, pl.ds(pl.multiple_of(col, tile), tile)],
            )
            total = part if total is None else total + part
        return total

    def send_results(a, c):
        for d in (3, 1, 2):
            for copy in plane_copies(True, a, c, d):
                copy.start()

    def forward_hidden():
        wait_packed(FWD)

        @pl.loop(0, ff // tile)
        def _(t):
            at = pl.multiple_of(t * tile, tile)
            g = in_dot(FWD, at)
            u = in_dot(FWD, ff + at)
            pre[:, pl.ds(at, tile)] = (jax.nn.silu(g) * u).astype(BF)

    def forward_out():
        wait_pack_sent(FWD)
        for c in range(chunks):

            @pl.loop(0, cw // tile)
            def _(t):
                at = pl.multiple_of(t * tile, tile)
                part = mm(pre[:, :ff], w_out[:, pl.ds(pl.multiple_of(c * cw + at, tile), tile)]).astype(BF)
                pack_x[FWD, c, :, :, pl.ds(at, tile)] = part.reshape(GROUP, slots, tile)

            send_results(FWD, c)

    for i, (a, c) in enumerate(items):
        line_arrived(a, c)
        send_line(i + 2)
        for d in (3, 1, 2, 0):
            x = line_x[a, c].reshape(rows, cw)
            gates = place[FWD if a == FWD else BWD, d].astype(F32)
            chosen = jnp.where(gates > 0.0, 1.0, 0.0).astype(BF)
            packed = mm(chosen, x, TN).astype(BF)
            if d == 0:
                recv_x[a, c, j] = packed
            else:
                pack_x[a, c, plane_peer(d)] = packed
                for copy in plane_copies(False, a, c, d):
                    copy.start()
        if i:
            pass_on(False, *items[i - 1])
        if i == 2 * chunks - 1:
            for copy in copies_w:
                copy.wait()
            forward_hidden()
        if i == 2 * chunks:
            forward_out()
    pass_on(False, *items[-1])
    for c in range(chunks):
        pass_on(True, FWD, c)

    for d in range(1, n_line):
        table_copy(d, zi).wait_send()

    wait_packed(BWD)
    wait_packed(COT)

    @pl.loop(0, ff // tile)
    def _(t):
        at = pl.multiple_of(t * tile, tile)
        g = in_dot(BWD, at)
        u = in_dot(BWD, ff + at)
        grad = None
        for c in range(chunks):
            part = mm(
                recv_x[COT, c].reshape(many, cw), w_out[pl.ds(at, tile), c * cw : (c + 1) * cw], NT
            )
            grad = part if grad is None else grad + part
        sg = jax.nn.sigmoid(g)
        pre[:, pl.ds(at, tile)] = (grad * u * (sg * (1.0 + g * (1.0 - sg)))).astype(BF)
        pre[:, pl.ds(pl.multiple_of(ff + at, tile), tile)] = (grad * (g * sg)).astype(BF)

    wait_pack_sent(BWD)
    for c in range(chunks):

        @pl.loop(0, cw // tile)
        def _(t):
            at = pl.multiple_of(t * tile, tile)
            part = mm(pre[...], w_in[pl.ds(pl.multiple_of(c * cw + at, tile), tile), :], NT).astype(BF)
            pack_x[BWD, c, :, :, pl.ds(at, tile)] = part.reshape(GROUP, slots, tile)

        send_results(BWD, c)

    wait_pack_sent(COT)

    for a in (BWD, COT, FWD):
        for c in range(chunks):
            line_sent(a, c)

    for a in (FWD, BWD):
        for c in range(chunks):
            if a == FWD:
                pass_on(True, BWD, c)
            plane_wait(True, a, c)

            @pl.loop(0, n_line)
            def _(z):
                at = pl.multiple_of(z * tok, tok)
                total = mm(place[a, 0, pl.ds(at, tok)], pack_x[a, c, j])
                for d in range(1, GROUP):
                    total = total + mm(place[a, d, pl.ds(at, tok)], recv_r[a, c, plane_peer(d)])
                line_x[a, c, z] = total.astype(BF)

                @pl.when(z == zi)
                def _():
                    own_sum[a, c] = total

            for d in range(1, n_line):
                sum_copy(a, c, d).start()

    def summed(a):
        parts = []
        for c in range(chunks):
            total = own_sum[a, c]
            for d in range(1, n_line):
                sum_copy(a, c, d).wait_recv()
                total = total + recv_z[a, c, d - 1].astype(F32)
            parts.append(total)
        return jnp.concatenate(parts, axis=1)

    def out_copy(a, out, step):
        return pltpu.make_async_remote_copy(
            final.at[a], out, o_send.at[a], o_recv.at[a],
            device_id=dev(lax.rem(seg + step, n_seg), zi, j), device_id_type=MESH,
        )

    final[FWD] = (fwd_tokens[...].astype(F32) + summed(FWD)).astype(BF)
    onward = out_copy(FWD, out_f, 1)
    onward.start()
    norm_grad = summed(BWD)
    x = bwd_tokens[...].astype(F32)
    scale = rms_scale(x)
    based = x * scale
    scaled = norm_grad * gain
    final[BWD] = (
        cotangent[...].astype(F32)
        + scale * (scaled - based * jnp.mean(scaled * based, axis=-1, keepdims=True))
    ).astype(BF)
    back = out_copy(BWD, out_b, n_seg - 1)
    back.start()

    for a in (BWD, FWD):
        for c in range(chunks):
            plane_sent(True, a, c)
            via_copy(True, a, c).wait_send()
            for d in range(1, n_line):
                sum_copy(a, c, d).wait_send()
    back.wait()
    onward.wait()


def local(sizes, fwd_tokens, fwd_routes, fwd_gates, bwd_tokens, bwd_routes, bwd_gates, cotangent,
          norm_gain, weight_in, weight_out):
    n_seg, n_exp = sizes
    tok, width = fwd_tokens.shape
    top = fwd_routes.shape[1]
    w_first, w_second = weight_in[0, 0], weight_out[0, 0]
    ff = w_second.shape[0]
    n_line = n_exp // GROUP
    cap = max(2, min(tok, 9 * tok * top // (8 * n_exp)))
    slots = -(-cap * n_line // 16) * 16
    chunks = 4
    cw = width // chunks
    tile = 256
    lanes = -(-4 * n_exp // 128) * 128
    vmem = pl.BlockSpec(memory_space=pltpu.VMEM)
    anyw = pl.BlockSpec(memory_space=pl.ANY)
    dma = pltpu.SemaphoreType.DMA
    many = GROUP * slots
    return pl.pallas_call(
        functools.partial(kernel, (n_seg, n_exp, cap, tile)),
        out_shape=[jax.ShapeDtypeStruct((tok, width), BF)] * 2,
        in_specs=[vmem] * 8 + [anyw] * 2,
        out_specs=[anyw] * 2,
        scratch_shapes=[
            pltpu.VMEM(w_first.shape, BF),
            pltpu.VMEM(w_second.shape, BF),
            pltpu.VMEM((n_line, tok, lanes), F32),
            pltpu.VMEM((3, chunks, n_line, tok, cw), BF),
            pltpu.VMEM((3, chunks, GROUP, slots, cw), BF),
            pltpu.VMEM((3, chunks, GROUP, slots, cw), BF),
            pltpu.VMEM((2, chunks, GROUP, slots, cw), BF),
            pltpu.VMEM((2, chunks, n_line - 1, tok, cw), BF),
            pltpu.VMEM((2, GROUP, n_line * tok, slots), BF),
            pltpu.VMEM((many, 2 * ff), BF),
            pltpu.VMEM((2, chunks, tok, cw), F32),
            pltpu.VMEM((2, tok, width), BF),
            pltpu.VMEM((2, 3, chunks, slots, cw // 2), BF),
            dma((2,)),
            dma((n_line,)), dma((n_line,)),
            dma((3, chunks, n_line // 2)), dma((3, chunks, n_line)),
            dma((3, chunks, n_line // 2, n_line // 2)),
            dma((3, chunks, GROUP + 1)), dma((3, chunks, GROUP + 1)),
            dma((2, chunks, GROUP + 1)), dma((2, chunks, GROUP + 1)),
            dma((2, chunks, n_line)), dma((2, chunks, n_line)),
            dma((2,)), dma((2,)),
        ],
        compiler_params=pltpu.CompilerParams(
            collective_id=0, has_side_effects=True, vmem_limit_bytes=62 * 1024 * 1024
        ),
        cost_estimate=pl.CostEstimate(
            flops=2 * many * width * ff * 8, bytes_accessed=2 * width * ff * 3, transcendentals=0
        ),
    )(fwd_tokens, fwd_routes.T, fwd_gates.T, bwd_tokens, bwd_routes.T, bwd_gates.T, cotangent, norm_gain,
      w_first, w_second)


def solution(mesh):
    rows = P(("segment", "expert"), None)
    placed = (rows,) * 7 + (
        P("segment", None),
        P("segment", "expert", None, None),
        P("segment", "expert", None, None),
    )
    return jax.shard_map(
        functools.partial(local, (mesh.shape["segment"], mesh.shape["expert"])),
        mesh=mesh,
        in_specs=placed,
        out_specs=(rows, rows),
        check_vma=False,
    )
```
